128 devices in a mesh: dp: 8 (over x_hi, y), tensor: 16 (over z, x_lo, core).
Axes of the slice: x: 4 (x_hi: 2, x_lo: 2; x = x_hi * 2 + x_lo), y: 4, z: 4, core: 2. Of those that a mesh axis runs over, the one named last changes fastest.
Arguments:
- qkv_weight: bfloat16 [5120, 3584], P(('dp', 'tensor')), may hold values from -0.078125 to 0.078125
- out_weight: bfloat16 [2560, 5120], P(('dp', 'tensor')), may hold values from -0.125 to 0.125
- qkv_grad: bfloat16 [5120, 3584], P(('dp', 'tensor')), may hold values from -6 to 6
- out_grad: bfloat16 [2560, 5120], P(('dp', 'tensor')), may hold values from -6 to 6
- qkv_moment: float32 [5120, 3584], P(('dp', 'tensor')), may hold values from -2 to 2
- out_moment: float32 [2560, 5120], P(('dp', 'tensor')), may hold values from -2 to 2
- qkv_second: float32 [5120, 3584], P(('dp', 'tensor')), may hold values from 0.05 to 2
- out_second: float32 [2560, 5120], P(('dp', 'tensor')), may hold values from 0.05 to 2
- step_states: bfloat16 [4, 3072, 5120], P(None, 'dp', 'tensor'), may hold values from -6 to 6
- key_cache: bfloat16 [3072, 4, 320, 128], P(('dp', 'tensor')), may hold values from -1200 to 1200
- value_cache: bfloat16 [3072, 4, 320, 128], P(('dp', 'tensor')), may hold values from -6 to 6
- prompt_lengths: int32 [3072], P(('dp', 'tensor')), may hold values from 40 to 320, as said below
Outputs:
- qkv_updated: bfloat16 [5120, 3584], P(('dp', 'tensor'))
- out_updated: bfloat16 [2560, 5120], P(('dp', 'tensor'))
- qkv_moment_next: float32 [5120, 3584], P(('dp', 'tensor'))
- out_moment_next: float32 [2560, 5120], P(('dp', 'tensor'))
- qkv_second_next: float32 [5120, 3584], P(('dp', 'tensor'))
- out_second_next: float32 [2560, 5120], P(('dp', 'tensor'))
- step_outputs: bfloat16 [4, 3072, 5120], P(None, 'dp', 'tensor')
The draws below stay inside these ranges and needn't reach their ends.
Inputs may be any that keep to these rules, and one draw needn't show every extreme that they name: Prompt b's cache holds valid entries at positions below prompt_lengths[b]; some prompt fills all 320 positions.
All inputs are finite; a program needn't handle non-finite values.
Results may differ from the reference program's by a relative error of at most 0.0045.
The reference program's roundings to bfloat16 on the way count: a program that leaves them out, or rounds other values in their place, can miss the bound.
Values may be sent and summed in bfloat16 or wider, within the bound.
No kernel may reach another device: no remote copies, remote signals or barrier semaphores. Data moves between devices by JAX's collectives and lax.ppermute only.
A program may use at most 128 MiB of HBM per device.

```python
import math
import jax
import jax.numpy as jnp
from jax import lax

D = 5120
HEADS = 20
KV_HEADS = 4
HEAD_DIM = 128
STEPS = 4
CACHE = 320
PROMPT_DEV = 24
ATT = 2560
QKV = 3584
PROMPTS = 3072


def draw_key_cache(key, part):
    key = jax.random.fold_in(key, 3)
    normal_key = jax.random.fold_in(key, 0)
    normal_part = jnp.clip(jax.random.normal(normal_key, (PROMPTS, KV_HEADS, CACHE, HEAD_DIM), jnp.float32), -6.0, 6.0)
    return normal_part.astype(jnp.bfloat16)


def draw_prompt_lengths(key, part):
    key = jax.random.fold_in(key, 7)
    lengths_drawn = jax.random.randint(key, (PROMPTS,), CACHE // 8, CACHE + 1, dtype=jnp.int32)
    return lengths_drawn.at[0].set(CACHE)


def shard_levels(key, dims, cuts, low, high):
    level, own = 1.0, jax.random.fold_in(key, 6)
    for dim, shards_of in cuts:
        heights = jnp.exp(jax.random.uniform(jax.random.fold_in(own, dim), (shards_of,), jnp.float32, low / len(cuts), high / len(cuts)))
        level = level * jnp.repeat(heights, dims[dim] // shards_of).reshape([-1 if axis == dim else 1 for axis in range(len(dims))])
    return level


def scatter_about(key, extent, scale, reach, cuts=(), kind=jnp.bfloat16):
    array = jax.random.normal(key, extent, jnp.float32) * scale
    if len(cuts) > 0:
        array = shard_levels(key, extent, cuts, -0.22, 0.18) * array
    return jnp.clip(array, min=-reach, max=reach).astype(kind)


def setup_inputs(seed: int = 0) -> dict:
    splits = jax.random.split(jax.random.key(seed), 13)
    qkv_weight = scatter_about(splits[0], (D, QKV), D ** -0.5, 0.078125, ((0, 128),))
    out_weight = scatter_about(splits[1], (ATT, D), ATT ** -0.5, 0.125, ((0, 128),))
    qkv_grad = scatter_about(splits[2], (D, QKV), 1.0, 6.0, ((0, 128),))
    out_grad = scatter_about(splits[3], (ATT, D), 1.0, 6.0, ((0, 128),))
    qkv_moment = scatter_about(splits[4], (D, QKV), 0.3, 2.0, ((0, 128),), jnp.float32)
    out_moment = scatter_about(splits[5], (ATT, D), 0.3, 2.0, ((0, 128),), jnp.float32)
    qkv_second = jnp.clip(jnp.exp(math.log(2.0) - 3.6888794 * jax.random.uniform(splits[6], (D, QKV), jnp.float32) ** shard_levels(splits[6], (D, QKV), ((0, 128),), -0.2, 0.2)), 0.05, 2.0)
    out_second = jnp.clip(jnp.exp(math.log(2.0) - 3.6888794 * jax.random.uniform(splits[7], (ATT, D), jnp.float32) ** shard_levels(splits[7], (ATT, D), ((0, 128),), -0.2, 0.2)), 0.05, 2.0)
    step_states = scatter_about(splits[8], (STEPS, PROMPTS, D), 1.0, 6.0, ((1, 8), (2, 16)))
    key_cache = draw_key_cache(jax.random.fold_in(splits[12], 71), 0)
    value_cache = scatter_about(splits[10], (PROMPTS, KV_HEADS, CACHE, HEAD_DIM), 1.0, 6.0, ((0, 128),))
    prompt_lengths = draw_prompt_lengths(jax.random.fold_in(splits[12], 71), 0)
    return dict(qkv_weight=qkv_weight, out_weight=out_weight, qkv_grad=qkv_grad, out_grad=out_grad, qkv_moment=qkv_moment, out_moment=out_moment, qkv_second=qkv_second, out_second=out_second, step_states=step_states, key_cache=key_cache, value_cache=value_cache, prompt_lengths=prompt_lengths)


beta_first = 0.9
beta_second = 0.95
learning_rate = 0.002
weight_decay = 0.1
adam_epsilon = 1e-08
bias_first = 1.0 - 0.9 ** 10
bias_second = 1.0 - 0.95 ** 10
norm_epsilon = 1e-06
rope_base = 1000000.0

def adam_update(param, grad, moment, second):
    param_wide = param.astype(jnp.float32)
    grad_wide = grad.astype(jnp.float32)
    moment_next = beta_first * moment + (1.0 - beta_first) * grad_wide
    second_next = beta_second * second + (1.0 - beta_second) * grad_wide * grad_wide
    moment_hat = moment_next / bias_first
    second_hat = second_next / bias_second
    updated = param_wide - learning_rate * (moment_hat / (jnp.sqrt(second_hat) + adam_epsilon) + weight_decay * param_wide)
    return (updated.astype(jnp.bfloat16), moment_next, second_next)

def rms_norm(states):
    widened = states.astype(jnp.float32)
    factor = lax.rsqrt(lax.optimization_barrier(jnp.mean(widened * widened, axis=-1, keepdims=True)) + norm_epsilon)
    return (widened * factor).astype(jnp.bfloat16)

def rotate(heads_in, positions):
    half_dim = HEAD_DIM // 2
    frequencies = rope_base ** (-2.0 * jnp.arange(half_dim, dtype=jnp.float32) / HEAD_DIM)
    angles = positions.astype(jnp.float32)[:, None] * frequencies[None, :]
    cosine = jnp.cos(angles)[:, None, :]
    sine_part = jnp.sin(angles)[:, None, :]
    widened = heads_in.astype(jnp.float32)
    front_half = widened[..., :half_dim]
    back_half = widened[..., half_dim:]
    return jnp.concatenate([front_half * cosine - back_half * sine_part, back_half * cosine + front_half * sine_part], axis=-1)

def attend(queries, cache_keys, cache_values, fresh_keys, fresh_values, lengths, step_index):
    prompt_count = queries.shape[0]
    score_scale = HEAD_DIM ** (-0.5)
    grouped = queries.reshape(prompt_count, KV_HEADS, HEADS // KV_HEADS, HEAD_DIM).astype(jnp.float32)
    cache_scores = jnp.einsum('pkgd,pkld->pkgl', grouped, cache_keys.astype(jnp.float32)) * score_scale
    fresh_scores = jnp.einsum('pkgd,pksd->pkgs', grouped, fresh_keys.astype(jnp.float32)) * score_scale
    cache_mask = (jnp.arange(cache_keys.shape[2])[None, :] < lengths[:, None])[:, None, None, :]
    fresh_mask = (jnp.arange(fresh_keys.shape[2]) <= step_index)[None, None, None, :]
    cache_scores = jnp.where(cache_mask, cache_scores, -1e+30)
    fresh_scores = jnp.where(fresh_mask, fresh_scores, -1e+30)
    largest = jnp.maximum(lax.optimization_barrier(jnp.max(cache_scores, axis=-1, keepdims=True)), lax.optimization_barrier(jnp.max(fresh_scores, axis=-1, keepdims=True)))
    cache_exp = jnp.exp(cache_scores - largest)
    fresh_exp = jnp.exp(fresh_scores - largest)
    denominator = lax.optimization_barrier(jnp.sum(cache_exp, axis=-1, keepdims=True)) + lax.optimization_barrier(jnp.sum(fresh_exp, axis=-1, keepdims=True))
    cache_weights = (cache_exp / denominator).astype(jnp.bfloat16)
    fresh_weights = (fresh_exp / denominator).astype(jnp.bfloat16)
    result = jnp.einsum('pkgl,pkld->pkgd', cache_weights.astype(jnp.float32), cache_values.astype(jnp.float32))
    result = result + jnp.einsum('pkgs,pksd->pkgd', fresh_weights.astype(jnp.float32), fresh_values.astype(jnp.float32))
    return result.reshape(prompt_count, HEADS * HEAD_DIM).astype(jnp.bfloat16)

def reference(qkv_weight, out_weight, qkv_grad, out_grad, qkv_moment, out_moment, qkv_second, out_second, step_states, key_cache, value_cache, prompt_lengths):
    qkv_updated, qkv_moment_next, qkv_second_next = adam_update(qkv_weight, qkv_grad, qkv_moment, qkv_second)
    out_updated, out_moment_next, out_second_next = adam_update(out_weight, out_grad, out_moment, out_second)
    att_width = HEADS * HEAD_DIM
    kv_width = KV_HEADS * HEAD_DIM
    prompt_count = key_cache.shape[0]
    block_count = prompt_count // PROMPT_DEV
    fresh_keys = jnp.zeros((prompt_count, KV_HEADS, STEPS, HEAD_DIM), jnp.bfloat16)
    fresh_values = jnp.zeros((prompt_count, KV_HEADS, STEPS, HEAD_DIM), jnp.bfloat16)
    cache_blocks = key_cache.reshape(block_count, PROMPT_DEV, KV_HEADS, key_cache.shape[2], HEAD_DIM)
    value_blocks = value_cache.reshape(block_count, PROMPT_DEV, KV_HEADS, key_cache.shape[2], HEAD_DIM)
    length_blocks = prompt_lengths.reshape(block_count, PROMPT_DEV)
    outputs = []
    for step_index in range(STEPS):
        states = step_states[step_index]
        normed = rms_norm(states)
        projected = jnp.dot(normed, qkv_updated, preferred_element_type=jnp.float32).astype(jnp.bfloat16)
        positions = prompt_lengths + step_index
        queries = rotate(projected[:, :att_width].reshape(prompt_count, HEADS, HEAD_DIM), positions).astype(jnp.bfloat16)
        keys_now = rotate(projected[:, att_width:att_width + kv_width].reshape(prompt_count, KV_HEADS, HEAD_DIM), positions).astype(jnp.bfloat16)
        values_now = projected[:, att_width + kv_width:].reshape(prompt_count, KV_HEADS, HEAD_DIM)
        fresh_keys = fresh_keys.at[:, :, step_index, :].set(keys_now)
        fresh_values = fresh_values.at[:, :, step_index, :].set(values_now)

        def one_block(pieces):
            return attend(pieces[0], pieces[1], pieces[2], pieces[3], pieces[4], pieces[5], step_index)
        attended = lax.map(one_block, (queries.reshape(block_count, PROMPT_DEV, HEADS, HEAD_DIM), cache_blocks, value_blocks, fresh_keys.reshape(block_count, PROMPT_DEV, KV_HEADS, STEPS, HEAD_DIM), fresh_values.reshape(block_count, PROMPT_DEV, KV_HEADS, STEPS, HEAD_DIM), length_blocks))
        attended = attended.reshape(prompt_count, att_width)
        projected_out = jnp.dot(attended, out_updated, preferred_element_type=jnp.float32)
        outputs.append((states.astype(jnp.float32) + projected_out).astype(jnp.bfloat16))
    return (qkv_updated, out_updated, qkv_moment_next, out_moment_next, qkv_second_next, out_second_next, jnp.stack(outputs))
```

```python
import jax
import jax.numpy as jnp
from jax import lax
from jax.experimental import pallas as pl
from jax.experimental.pallas import tpu as pltpu
from jax.sharding import Mesh
from jax.sharding import PartitionSpec as P

D = 5120
HEADS = 20
KV_HEADS = 4
HEAD_DIM = 128
STEPS = 4
GROUP = HEADS // KV_HEADS
ATT = HEADS * HEAD_DIM
KV = KV_HEADS * HEAD_DIM
QKV = ATT + 2 * KV
PROMPT_DEV = 24
CACHE = 320
ROWS = STEPS * PROMPT_DEV
QKV_COLS = QKV // 4
OUT_COLS = D // 4
FEATURES = D // 16

beta_first = 0.9
beta_second = 0.95
learning_rate = 0.002
weight_decay = 0.1
adam_epsilon = 1e-08
bias_first = 1.0 - 0.9**10
bias_second = 1.0 - 0.95**10
norm_epsilon = 1e-06
rope_base = 1000000.0

SIZES = (2, 4, 4, 2, 2)
AXES = ("xh", "y", "z", "xl", "c")


def adam_update(param, grad, moment, second):
    param_wide = param.astype(jnp.float32)
    grad_wide = grad.astype(jnp.float32)
    moment_next = beta_first * moment + (1.0 - beta_first) * grad_wide
    second_next = beta_second * second + (1.0 - beta_second) * grad_wide * grad_wide
    moment_hat = moment_next / bias_first
    second_hat = second_next / bias_second
    updated = param_wide - learning_rate * (
        moment_hat / (jnp.sqrt(second_hat) + adam_epsilon) + weight_decay * param_wide
    )
    return (updated.astype(jnp.bfloat16), moment_next, second_next)


def device_of(x, y, z, c):
    return ((((x // 2) * 4 + y) * 4 + z) * 2 + x % 2) * 2 + c


def plane_pairs(phase, shift):
    pairs = []
    for x in range(4):
        for y in range(4):
            for z in range(4):
                for c in range(2):
                    if c == phase:
                        target = device_of((x + shift) % 4, y, z, c)
                    else:
                        target = device_of(x, (y + shift) % 4, z, c)
                    pairs.append((device_of(x, y, z, c), target))
    return pairs


def plane_permute(array, phase, shift):
    return lax.ppermute(array, AXES, plane_pairs(phase, shift))


def z_permute(array, shift):
    return lax.ppermute(array, "z", [(j, (j + shift) % 4) for j in range(4)])


def core_permute(array):
    return lax.ppermute(array, "c", [(0, 1), (1, 0)])


def z_ring(array, half):
    below = z_permute(array, 1)
    above = z_permute(array, -1)
    return below, above, z_permute(below[:half], 1), z_permute(above[half:], -1)


def plane_gather(block):
    first = jnp.stack(
        [
            block,
            plane_permute(block, 0, 1),
            plane_permute(block, 0, 2),
            plane_permute(block, 0, -1),
        ]
    )
    below = plane_permute(first, 1, 1)
    above = plane_permute(first, 1, -1)
    own = (first, below, plane_permute(below[:2], 1, 1), plane_permute(above[2:], 1, -1), above)
    return own + tuple(core_permute(piece) for piece in own)


def fetch(piece_refs, held, sems):
    copies = []
    for who in range(2):
        first, below, far_low, far_high, above = piece_refs[5 * who : 5 * who + 5]
        places = (
            (first, held.at[who, 0]),
            (below, held.at[who, 1]),
            (far_low, held.at[who, 2, pl.ds(0, 2)]),
            (far_high, held.at[who, 2, pl.ds(2, 2)]),
            (above, held.at[who, 3]),
        )
        for index, (source, place) in enumerate(places):
            copies.append(pltpu.make_async_copy(source, place, sems.at[5 * who + index]))
    for copy in copies:
        copy.start()
    return copies


def held_block(held, pos_ref, core_type, x_from, y_from, z_from):
    x_back = (pos_ref[0] - x_from) & 3
    y_back = (pos_ref[1] - y_from) & 3
    z_back = (pos_ref[2] - z_from) & 3
    who = pos_ref[3] ^ core_type
    if core_type == 0:
        block = held[who, y_back, x_back, z_back]
    else:
        block = held[who, x_back, y_back, z_back]
    return block.astype(jnp.float32)


def project_kernel(
    pos_ref, x0, x1, x2_low, x2_high, x3, *rest
):
    piece_refs = rest[:10]
    out_ref, held, weight, sems = rest[10:]
    copies = fetch(piece_refs, held, sems)
    for copy in copies:
        copy.wait()

    def place(index, carry):
        d, z_from, xl = index // 8, (index // 2) & 3, index & 1
        x_from, y_from = (d // 4) * 2 + xl, d & 3
        pair = jnp.concatenate(
            [held_block(held, pos_ref, ct, x_from, y_from, z_from) for ct in range(2)], axis=0
        )
        weight[pl.ds(pl.multiple_of(index * 80, 80), 80), :] = pair.astype(jnp.bfloat16)
        return carry

    lax.fori_loop(0, 64, place, 0)
    z = pos_ref[2]
    for half in range(2):
        rows = pl.ds(half * 2 * ROWS, 2 * ROWS)
        parts = [x0[rows, :], x1[rows, :], (x2_low if half == 0 else x2_high)[...], x3[rows, :]]
        parts = [part.astype(jnp.float32) for part in parts]
        total = sum(jnp.sum(part * part, axis=-1, keepdims=True) for part in parts)
        factor = lax.rsqrt(total / D + norm_epsilon)
        result = None
        for back, part in enumerate(parts):
            start = pl.multiple_of(((z - back) & 3) * OUT_COLS, OUT_COLS)
            term = jnp.dot(
                (part * factor).astype(jnp.bfloat16),
                weight[pl.ds(start, OUT_COLS), :],
                preferred_element_type=jnp.float32,
            )
            result = term if result is None else result + term
        result = result.astype(jnp.bfloat16)
        for inner in range(2):
            out_ref[(2 * half + inner - z) & 3] = result[inner * ROWS : (inner + 1) * ROWS]


def output_kernel(pos_ref, a0, a1, a2_low, a2_high, a3, states, *rest):
    piece_refs = rest[:10]
    out_ref, held, weight, sems = rest[10:]
    copies = fetch(piece_refs, held, sems)
    for copy in copies:
        copy.wait()

    def place(index, carry):
        d, z_from = index // 4, index & 3
        x_from, y_from = (d // 4) * 2, d & 3
        for ct in range(2):
            pair = jnp.concatenate(
                [held_block(held, pos_ref, ct, x_from + xl, y_from, z_from) for xl in range(2)],
                axis=0,
            )
            weight[pl.ds(pl.multiple_of(index * 80, 80), 80), ct * 640 : ct * 640 + 640] = (
                pair.astype(jnp.bfloat16)
            )
        return carry

    lax.fori_loop(0, 32, place, 0)
    z = pos_ref[2]
    parts = [
        a0[...],
        a1[...],
        jnp.concatenate([a2_low[...], a2_high[...]], axis=0),
        a3[...],
    ]
    for back, part in enumerate(parts):
        owner = (z - back) & 3
        rows = pl.ds(pl.multiple_of(owner * ROWS, ROWS), ROWS)
        result = jnp.dot(part, weight[...], preferred_element_type=jnp.float32)
        result = (states[rows, :].astype(jnp.float32) + result).astype(jnp.bfloat16)
        for block in range(4):
            out_ref[block, owner] = result[:, block * FEATURES : (block + 1) * FEATURES]


def call_kernel(kernel, out_shape, columns, depth, vmem_count, flops, *operands):
    vmem = pl.BlockSpec(memory_space=pltpu.VMEM)
    return pl.pallas_call(
        kernel,
        out_shape=out_shape,
        in_specs=[pl.BlockSpec(memory_space=pltpu.SMEM)]
        + [vmem] * vmem_count
        + [pl.BlockSpec(memory_space=pl.ANY)] * 10,
        out_specs=vmem,
        scratch_shapes=[
            pltpu.VMEM((2, 4, 4, 4, 40, columns), jnp.bfloat16),
            pltpu.VMEM(depth, jnp.bfloat16),
            pltpu.SemaphoreType.DMA((10,)),
        ],
        compiler_params=pltpu.CompilerParams(vmem_limit_bytes=44 * 1024 * 1024),
        cost_estimate=pl.CostEstimate(
            flops=flops, bytes_accessed=24 * 1024 * 1024, transcendentals=0
        ),
    )(*operands)


def rotate(heads_in, cosine, sine_part):
    half_dim = HEAD_DIM // 2
    widened = heads_in.astype(jnp.float32)
    front_half = widened[..., :half_dim]
    back_half = widened[..., half_dim:]
    return jnp.concatenate(
        [front_half * cosine - back_half * sine_part, back_half * cosine + front_half * sine_part],
        axis=-1,
    ).astype(jnp.bfloat16)


def attend(projected, key_cache, value_cache, lengths):
    half_dim = HEAD_DIM // 2
    frequencies = rope_base ** (-2.0 * jnp.arange(half_dim, dtype=jnp.float32) / HEAD_DIM)
    positions = lengths[None, :] + jnp.arange(STEPS, dtype=jnp.int32)[:, None]
    angles = positions.astype(jnp.float32)[:, :, None] * frequencies
    cosine, sine_part = jnp.cos(angles)[:, :, None, :], jnp.sin(angles)[:, :, None, :]
    heads = projected.reshape(STEPS, PROMPT_DEV, HEADS + 2 * KV_HEADS, HEAD_DIM)
    rotated = rotate(heads[:, :, : HEADS + KV_HEADS], cosine, sine_part)
    queries = rotated[:, :, :HEADS].reshape(STEPS, PROMPT_DEV, KV_HEADS, GROUP, HEAD_DIM)
    queries = queries.transpose(1, 2, 0, 3, 4).reshape(
        PROMPT_DEV, KV_HEADS, STEPS * GROUP, HEAD_DIM
    )
    fresh_keys = rotated[:, :, HEADS:].transpose(1, 2, 0, 3)
    fresh_values = heads[:, :, HEADS + KV_HEADS :].transpose(1, 2, 0, 3)
    score_scale = HEAD_DIM ** (-0.5)
    cache_scores = (
        jnp.einsum("pkgd,pkld->pkgl", queries, key_cache, preferred_element_type=jnp.float32)
        * score_scale
    )
    fresh_scores = (
        jnp.einsum("pkgd,pksd->pkgs", queries, fresh_keys, preferred_element_type=jnp.float32)
        * score_scale
    )
    cache_mask = (jnp.arange(CACHE)[None, :] < lengths[:, None])[:, None, None, :]
    row_step = jnp.arange(STEPS * GROUP) // GROUP
    fresh_mask = (jnp.arange(STEPS)[None, :] <= row_step[:, None])[None, None]
    cache_scores = jnp.where(cache_mask, cache_scores, -1e30)
    fresh_scores = jnp.where(fresh_mask, fresh_scores, -1e30)
    largest = jnp.maximum(
        jnp.max(cache_scores, axis=-1, keepdims=True), jnp.max(fresh_scores, axis=-1, keepdims=True)
    )
    cache_exp = jnp.exp(cache_scores - largest)
    fresh_exp = jnp.exp(fresh_scores - largest)
    denominator = jnp.sum(cache_exp, axis=-1, keepdims=True) + jnp.sum(
        fresh_exp, axis=-1, keepdims=True
    )
    cache_weights = (cache_exp / denominator).astype(jnp.bfloat16)
    fresh_weights = (fresh_exp / denominator).astype(jnp.bfloat16)
    result = jnp.einsum(
        "pkgl,pkld->pkgd", cache_weights, value_cache, preferred_element_type=jnp.float32
    )
    result = result + jnp.einsum(
        "pkgs,pksd->pkgd", fresh_weights, fresh_values, preferred_element_type=jnp.float32
    )
    result = result.reshape(PROMPT_DEV, KV_HEADS, STEPS, GROUP, HEAD_DIM).transpose(2, 0, 1, 3, 4)
    return result.reshape(ROWS, ATT).astype(jnp.bfloat16)


def on_device(
    qkv_weight,
    out_weight,
    qkv_grad,
    out_grad,
    qkv_moment,
    out_moment,
    qkv_second,
    out_second,
    step_states,
    key_cache,
    value_cache,
    prompt_lengths,
):
    xh, y, z, xl, c = (lax.axis_index(axis) for axis in AXES)
    place = xl * 2 + c
    position = jnp.stack([xh * 2 + xl, y, z, c]).astype(jnp.int32)

    def trade(block_to):
        came = [block_to(place)]
        for other in range(1, 4):
            came.append(
                lax.ppermute(
                    block_to(place ^ other), ("xl", "c"), [(i, i ^ other) for i in range(4)]
                )
            )
        return [lax.select_n(place, *[came[i ^ j] for j in range(4)]) for i in range(4)]

    qkv_updated, qkv_moment_next, qkv_second_next = adam_update(
        qkv_weight, qkv_grad, qkv_moment, qkv_second
    )
    out_updated, out_moment_next, out_second_next = adam_update(
        out_weight, out_grad, out_moment, out_second
    )

    by_place = step_states.reshape(STEPS, 4, 4, PROMPT_DEV, FEATURES)
    by_place = by_place.transpose(2, 1, 0, 3, 4).reshape(4, 4 * ROWS, FEATURES)
    own_states = jnp.concatenate(
        trade(lambda i: lax.dynamic_index_in_dim(by_place, i, 0, keepdims=False)), axis=-1
    )
    x_below, x_above, x_far_low, x_far_high = z_ring(own_states, 2 * ROWS)

    qkv_block = [
        z_permute(
            lax.dynamic_slice_in_dim(qkv_updated, ((z + shift) % 4) * QKV_COLS, QKV_COLS, 1), shift
        )
        for shift in range(1, 4)
    ]
    qkv_block = [lax.dynamic_slice_in_dim(qkv_updated, z * QKV_COLS, QKV_COLS, 1)] + qkv_block
    qkv_pieces = plane_gather(jnp.stack(qkv_block))
    projected = call_kernel(
        project_kernel,
        jax.ShapeDtypeStruct((4, ROWS, QKV_COLS), jnp.bfloat16),
        QKV_COLS,
        (D, QKV_COLS),
        5,
        2 * 4 * ROWS * D * QKV_COLS,
        position,
        own_states,
        x_below,
        x_far_low,
        x_far_high,
        x_above,
        *qkv_pieces,
    )

    halves = out_updated.reshape(20, 4, 2, OUT_COLS // 2)
    own_half = lax.dynamic_index_in_dim(halves, c, 2, keepdims=False)
    other_half = core_permute(lax.dynamic_index_in_dim(halves, 1 - c, 2, keepdims=False))
    both = jnp.where(
        c == 0,
        jnp.concatenate([own_half, other_half], axis=0),
        jnp.concatenate([other_half, own_half], axis=0),
    ).transpose(1, 0, 2)
    out_block = [lax.dynamic_index_in_dim(both, z, 0, keepdims=False)] + [
        z_permute(lax.dynamic_index_in_dim(both, (z + shift) % 4, 0, keepdims=False), shift)
        for shift in range(1, 4)
    ]
    out_pieces = plane_gather(jnp.stack(out_block))

    columns = [projected[0]] + [z_permute(projected[shift], shift) for shift in range(1, 4)]
    own_rows = jnp.concatenate(
        [lax.select_n(z, *[columns[(j - i) % 4] for j in range(4)]) for i in range(4)], axis=-1
    )
    attended = attend(own_rows, key_cache, value_cache, prompt_lengths)
    a_below, a_above, a_far_low, a_far_high = z_ring(attended, ROWS // 2)
    blocks = call_kernel(
        output_kernel,
        jax.ShapeDtypeStruct((4, 4, ROWS, FEATURES), jnp.bfloat16),
        OUT_COLS // 2,
        (ATT, OUT_COLS),
        6,
        2 * 4 * ROWS * ATT * OUT_COLS,
        position,
        attended,
        a_below,
        a_far_low,
        a_far_high,
        a_above,
        own_states,
        *out_pieces,
    )
    came = trade(lambda i: lax.dynamic_index_in_dim(blocks, i, 0, keepdims=False))
    outputs = jnp.stack(
        [block.reshape(4, STEPS, PROMPT_DEV, FEATURES) for block in came], axis=1
    )
    outputs = outputs.transpose(2, 0, 1, 3, 4).reshape(STEPS, 16 * PROMPT_DEV, FEATURES)
    return (
        qkv_updated,
        out_updated,
        qkv_moment_next,
        out_moment_next,
        qkv_second_next,
        out_second_next,
        outputs,
    )


def solution(mesh):
    fine = Mesh(mesh.devices.reshape(SIZES), AXES)
    rows = P(AXES, None)
    caches = P(AXES, None, None, None)
    states = P(None, ("xh", "y"), ("z", "xl", "c"))
    return jax.shard_map(
        on_device,
        mesh=fine,
        in_specs=(rows,) * 8 + (states, caches, caches, P(AXES)),
        out_specs=(rows,) * 6 + (states,),
        check_vma=False,
    )
```

```python
import jax
import jax.numpy as jnp
from jax import lax
from jax.experimental import pallas as pl
from jax.experimental.pallas import tpu as pltpu
from jax.sharding import Mesh
from jax.sharding import PartitionSpec as P

D = 5120
HEADS = 20
KV_HEADS = 4
HEAD_DIM = 128
STEPS = 4
GROUP = HEADS // KV_HEADS
ATT = HEADS * HEAD_DIM
KV = KV_HEADS * HEAD_DIM
QKV = ATT + 2 * KV
PROMPT_DEV = 24
CACHE = 320
ROWS = STEPS * PROMPT_DEV
QKV_COLS = QKV // 4
OUT_COLS = D // 4
FEATURES = D // 16

beta_first = 0.9
beta_second = 0.95
learning_rate = 0.002
weight_decay = 0.1
adam_epsilon = 1e-08
bias_first = 1.0 - 0.9**10
bias_second = 1.0 - 0.95**10
norm_epsilon = 1e-06
rope_base = 1000000.0

SIZES = (2, 4, 4, 2, 2)
AXES = ("xh", "y", "z", "xl", "c")


def adam_update(param, grad, moment, second):
    param_wide = param.astype(jnp.float32)
    grad_wide = grad.astype(jnp.float32)
    moment_next = beta_first * moment + (1.0 - beta_first) * grad_wide
    second_next = beta_second * second + (1.0 - beta_second) * grad_wide * grad_wide
    moment_hat = moment_next / bias_first
    second_hat = second_next / bias_second
    updated = param_wide - learning_rate * (
        moment_hat / (jnp.sqrt(second_hat) + adam_epsilon) + weight_decay * param_wide
    )
    return (updated.astype(jnp.bfloat16), moment_next, second_next)


def device_of(x, y, z, c):
    return ((((x // 2) * 4 + y) * 4 + z) * 2 + x % 2) * 2 + c


def plane_pairs(phase, shift):
    pairs = []
    for x in range(4):
        for y in range(4):
            for z in range(4):
                for c in range(2):
                    if c == phase:
                        target = device_of((x + shift) % 4, y, z, c)
                    else:
                        target = device_of(x, (y + shift) % 4, z, c)
                    pairs.append((device_of(x, y, z, c), target))
    return pairs


def plane_permute(array, phase, shift):
    return lax.ppermute(array, AXES, plane_pairs(phase, shift))


def z_permute(array, shift):
    return lax.ppermute(array, "z", [(j, (j + shift) % 4) for j in range(4)])


def core_permute(array):
    return lax.ppermute(array, "c", [(0, 1), (1, 0)])


def z_ring(low, high):
    low_1, high_3 = z_permute(low, 1), z_permute(high, -1)
    high_1, low_3 = z_permute(high, 1), z_permute(low, -1)
    low_2, high_2 = z_permute(low_1, 1), z_permute(high_3, -1)
    return (low_1, low_2, low_3), (high_1, high_2, high_3)


def plane_gather(block):
    first = jnp.stack(
        [
            block,
            plane_permute(block, 0, 1),
            plane_permute(block, 0, 2),
            plane_permute(block, 0, -1),
        ]
    )
    return (first,) + tuple(plane_permute(first, 1, shift) for shift in (1, 2, -1))


def fetch(piece_refs, held, sems):
    copies = [
        pltpu.make_async_copy(piece, held.at[index // 4, index % 4], sems.at[index])
        for index, piece in enumerate(piece_refs)
    ]
    for copy in copies:
        copy.start()
    for copy in copies:
        copy.wait()


def held_block(held, pos_ref, core_type, x_from, y_from, z_from):
    x_back = (pos_ref[0] - x_from) & 3
    y_back = (pos_ref[1] - y_from) & 3
    z_back = (pos_ref[2] - z_from) & 3
    who = pos_ref[3] ^ core_type
    if core_type == 0:
        block = held[who, y_back, x_back, z_back]
    else:
        block = held[who, x_back, y_back, z_back]
    return block.astype(jnp.float32)


def project_kernel(pos_ref, *refs):
    states, piece_refs, outs = refs[0], refs[1:9], refs[9:13]
    held, weight, by_shift, sems = refs[13:]
    fetch(piece_refs, held, sems)

    def place(index, carry):
        d, z_from, xl = index // 8, (index // 2) & 3, index & 1
        x_from, y_from = (d // 4) * 2 + xl, d & 3
        pair = jnp.concatenate(
            [held_block(held, pos_ref, ct, x_from, y_from, z_from) for ct in range(2)], axis=0
        )
        weight[pl.ds(pl.multiple_of(index * 80, 80), 80), :] = pair.astype(jnp.bfloat16)
        return carry

    lax.fori_loop(0, 64, place, 0)
    z = pos_ref[2]
    for half in range(2):
        rows = pl.ds(half * 2 * ROWS, 2 * ROWS)
        parts = [states[block, rows, :].astype(jnp.float32) for block in range(4)]
        total = sum(jnp.sum(part * part, axis=-1, keepdims=True) for part in parts)
        factor = lax.rsqrt(total / D + norm_epsilon)
        result = None
        for block, part in enumerate(parts):
            term = jnp.dot(
                (part * factor).astype(jnp.bfloat16),
                weight[block * OUT_COLS : (block + 1) * OUT_COLS, :],
                preferred_element_type=jnp.float32,
            )
            result = term if result is None else result + term
        result = result.astype(jnp.bfloat16)
        for inner in range(2):
            by_shift[(2 * half + inner - z) & 3] = result[inner * ROWS : (inner + 1) * ROWS]
    for shift in range(4):
        outs[shift][...] = by_shift[shift]


def order_kernel(halves_ref, weight, held, sem):
    copy = pltpu.make_async_copy(halves_ref, held, sem)
    copy.start()
    copy.wait()

    def place(index, carry):
        d, z_from = index // 4, index & 3
        for half in range(2):
            pair = jnp.concatenate(
                [held[d // 4, d & 3, xl, half, z_from].astype(jnp.float32) for xl in range(2)],
                axis=0,
            )
            weight[
                pl.ds(pl.multiple_of(index * 80, 80), 80),
                half * OUT_COLS // 2 : (half + 1) * OUT_COLS // 2,
            ] = pair.astype(jnp.bfloat16)
        return carry

    lax.fori_loop(0, 32, place, 0)


def output_kernel(pos_ref, *refs):
    lows, highs, states, weight, out_ref = refs[:4], refs[4:8], refs[8], refs[9], refs[10]
    z = pos_ref[2]
    for back in range(4):
        owner = (z - back) & 3
        part = jnp.concatenate([lows[back][...], highs[back][...]], axis=0)
        result = jnp.dot(part, weight[...], preferred_element_type=jnp.float32)
        rows = pl.ds(pl.multiple_of(owner * ROWS, ROWS), ROWS)
        result = (states[rows, :].astype(jnp.float32) + result).astype(jnp.bfloat16)
        for block in range(4):
            out_ref[block, owner] = result[:, block * FEATURES : (block + 1) * FEATURES]


SMEM_SPEC = pl.BlockSpec(memory_space=pltpu.SMEM)
VMEM_SPEC = pl.BlockSpec(memory_space=pltpu.VMEM)
ANY_SPEC = pl.BlockSpec(memory_space=pl.ANY)


def bf16(*shape):
    return jax.ShapeDtypeStruct(shape, jnp.bfloat16)


def params(mebibytes):
    return pltpu.CompilerParams(vmem_limit_bytes=mebibytes * 1024 * 1024)


def cost(flops, size):
    return pl.CostEstimate(flops=flops, bytes_accessed=size, transcendentals=0)


def project(position, states, pieces):
    return pl.pallas_call(
        project_kernel,
        out_shape=[bf16(ROWS, QKV_COLS)] * 4,
        in_specs=[SMEM_SPEC, VMEM_SPEC] + [ANY_SPEC] * 8,
        out_specs=[VMEM_SPEC] * 4,
        scratch_shapes=[
            pltpu.VMEM((2, 4, 4, 4, 40, QKV_COLS), jnp.bfloat16),
            pltpu.VMEM((D, QKV_COLS), jnp.bfloat16),
            pltpu.VMEM((4, ROWS, QKV_COLS), jnp.bfloat16),
            pltpu.SemaphoreType.DMA((8,)),
        ],
        compiler_params=params(40),
        cost_estimate=cost(8 * ROWS * D * QKV_COLS, 20000000),
    )(position, states, *pieces)


def order(halves):
    return pl.pallas_call(
        order_kernel,
        out_shape=bf16(ATT, OUT_COLS),
        in_specs=[ANY_SPEC],
        out_specs=VMEM_SPEC,
        scratch_shapes=[
            pltpu.VMEM(halves.shape, jnp.bfloat16),
            pltpu.SemaphoreType.DMA(()),
        ],
        compiler_params=params(24),
        cost_estimate=cost(0, 14000000),
    )(halves)


def project_out(position, lows, highs, states, weight):
    return pl.pallas_call(
        output_kernel,
        out_shape=bf16(4, 4, ROWS, FEATURES),
        in_specs=[SMEM_SPEC] + [VMEM_SPEC] * 10,
        out_specs=VMEM_SPEC,
        compiler_params=params(24),
        cost_estimate=cost(8 * ROWS * ATT * OUT_COLS, 12000000),
    )(position, *lows, *highs, states, weight)


def stack_kernel(*refs):
    for index in range(4):
        refs[5][index] = refs[index][:, :QKV_COLS]
        refs[6][index] = refs[index][:, QKV_COLS:]


def stack_blocks(blocks, states):
    return pl.pallas_call(
        stack_kernel,
        out_shape=[
            bf16(4, 40, QKV_COLS),
            bf16(4, 40, OUT_COLS // 2),
            jax.ShapeDtypeStruct(states.shape, states.dtype),
        ],
        in_specs=[VMEM_SPEC] * 4 + [ANY_SPEC],
        out_specs=[VMEM_SPEC] * 2 + [ANY_SPEC],
        input_output_aliases={4: 2},
    )(*blocks, states)


def halves_kernel(pos_ref, block_ref, *refs):
    c = pos_ref[3]
    for index in range(4):
        from_block = block_ref[(pos_ref[2] - index) & 3].astype(jnp.float32)
        low, high = from_block[:20], from_block[20:]
        refs[-2][index] = jnp.where(c == 0, low, high).astype(jnp.bfloat16)
        refs[-1][index] = jnp.where(c == 0, high, low).astype(jnp.bfloat16)


def halves_of(position, block, *after):
    return pl.pallas_call(
        halves_kernel,
        out_shape=[bf16(4, 20, OUT_COLS // 2)] * 2,
        in_specs=[SMEM_SPEC, VMEM_SPEC] + [ANY_SPEC] * len(after),
        out_specs=[VMEM_SPEC] * 2,
    )(position, block, *after)


def rotate(heads_in, cosine, sine_part):
    half_dim = HEAD_DIM // 2
    widened = heads_in.astype(jnp.float32)
    front_half = widened[..., :half_dim]
    back_half = widened[..., half_dim:]
    return jnp.concatenate(
        [front_half * cosine - back_half * sine_part, back_half * cosine + front_half * sine_part],
        axis=-1,
    ).astype(jnp.bfloat16)


def attend(projected, key_cache, value_cache, lengths):
    half_dim = HEAD_DIM // 2
    frequencies = rope_base ** (-2.0 * jnp.arange(half_dim, dtype=jnp.float32) / HEAD_DIM)
    positions = lengths[None, :] + jnp.arange(STEPS, dtype=jnp.int32)[:, None]
    angles = positions.astype(jnp.float32)[:, :, None] * frequencies
    cosine, sine_part = jnp.cos(angles)[:, :, None, :], jnp.sin(angles)[:, :, None, :]
    heads = projected.reshape(STEPS, PROMPT_DEV, HEADS + 2 * KV_HEADS, HEAD_DIM)
    rotated = rotate(heads[:, :, : HEADS + KV_HEADS], cosine, sine_part)
    queries = rotated[:, :, :HEADS].reshape(STEPS, PROMPT_DEV, KV_HEADS, GROUP, HEAD_DIM)
    queries = queries.transpose(1, 2, 0, 3, 4).reshape(
        PROMPT_DEV, KV_HEADS, STEPS * GROUP, HEAD_DIM
    )
    fresh_keys = rotated[:, :, HEADS:].transpose(1, 2, 0, 3)
    fresh_values = heads[:, :, HEADS + KV_HEADS :].transpose(1, 2, 0, 3)
    score_scale = HEAD_DIM ** (-0.5)
    cache_scores = (
        jnp.einsum("pkgd,pkld->pkgl", queries, key_cache, preferred_element_type=jnp.float32)
        * score_scale
    )
    fresh_scores = (
        jnp.einsum("pkgd,pksd->pkgs", queries, fresh_keys, preferred_element_type=jnp.float32)
        * score_scale
    )
    cache_mask = (jnp.arange(CACHE)[None, :] < lengths[:, None])[:, None, None, :]
    row_step = jnp.arange(STEPS * GROUP) // GROUP
    fresh_mask = (jnp.arange(STEPS)[None, :] <= row_step[:, None])[None, None]
    cache_scores = jnp.where(cache_mask, cache_scores, -1e30)
    fresh_scores = jnp.where(fresh_mask, fresh_scores, -1e30)
    largest = jnp.maximum(
        jnp.max(cache_scores, axis=-1, keepdims=True), jnp.max(fresh_scores, axis=-1, keepdims=True)
    )
    cache_exp = jnp.exp(cache_scores - largest)
    fresh_exp = jnp.exp(fresh_scores - largest)
    denominator = jnp.sum(cache_exp, axis=-1, keepdims=True) + jnp.sum(
        fresh_exp, axis=-1, keepdims=True
    )
    cache_weights = (cache_exp / denominator).astype(jnp.bfloat16)
    fresh_weights = (fresh_exp / denominator).astype(jnp.bfloat16)
    result = jnp.einsum(
        "pkgl,pkld->pkgd", cache_weights, value_cache, preferred_element_type=jnp.float32
    )
    result = result + jnp.einsum(
        "pkgs,pksd->pkgd", fresh_weights, fresh_values, preferred_element_type=jnp.float32
    )
    result = result.reshape(PROMPT_DEV, KV_HEADS, STEPS, GROUP, HEAD_DIM).transpose(2, 0, 1, 3, 4)
    return result.reshape(ROWS, ATT).astype(jnp.bfloat16)


def on_device(
    qkv_weight,
    out_weight,
    qkv_grad,
    out_grad,
    qkv_moment,
    out_moment,
    qkv_second,
    out_second,
    step_states,
    key_cache,
    value_cache,
    prompt_lengths,
):
    xh, y, z, xl, c = (lax.axis_index(axis) for axis in AXES)
    place = xl * 2 + c
    position = jnp.stack([xh * 2 + xl, y, z, c]).astype(jnp.int32)

    def trade(block_to):
        came = [block_to(place)]
        for other in range(1, 4):
            came.append(
                lax.ppermute(
                    block_to(place ^ other), ("xl", "c"), [(i, i ^ other) for i in range(4)]
                )
            )
        return [lax.select_n(place, *[came[i ^ j] for j in range(4)]) for i in range(4)]

    qkv_updated, qkv_moment_next, qkv_second_next = adam_update(
        qkv_weight, qkv_grad, qkv_moment, qkv_second
    )
    out_updated, out_moment_next, out_second_next = adam_update(
        out_weight, out_grad, out_moment, out_second
    )

    by_place = step_states.reshape(STEPS, 4, 4, PROMPT_DEV, FEATURES)
    by_place = by_place.transpose(2, 1, 0, 3, 4).reshape(4, 4 * ROWS, FEATURES)
    came = trade(lambda i: lax.dynamic_index_in_dim(by_place, i, 0, keepdims=False))
    own_states = jnp.concatenate(came, axis=-1)

    by_z = jnp.concatenate(
        [
            qkv_updated.reshape(40, 4, QKV_COLS).transpose(1, 0, 2),
            out_updated.reshape(20, 4, 2, OUT_COLS // 2)
            .transpose(1, 2, 0, 3)
            .reshape(4, 40, OUT_COLS // 2),
        ],
        axis=-1,
    )
    blocks = [lax.dynamic_index_in_dim(by_z, z, 0, keepdims=False)] + [
        z_permute(lax.dynamic_index_in_dim(by_z, (z + shift) & 3, 0, keepdims=False), shift)
        for shift in range(1, 4)
    ]
    qkv_block, out_block, own_states = stack_blocks(blocks, own_states)
    all_states = lax.all_gather(own_states, "z")
    qkv_pieces = plane_gather(qkv_block)
    qkv_pieces = qkv_pieces + tuple(core_permute(piece) for piece in qkv_pieces)
    projected = project(position, all_states, qkv_pieces)

    own_half, sent_half = halves_of(position, out_block, *qkv_pieces[1:4])
    other_half = core_permute(sent_half)
    both = jnp.where(
        c == 0,
        jnp.concatenate([own_half, other_half], axis=1),
        jnp.concatenate([other_half, own_half], axis=1),
    )
    gathered = lax.all_gather(both, ("xh", "y", "xl", "c"))
    out_columns = order(gathered.reshape(2, 4, 2, 2, 4, 40, OUT_COLS // 2))

    columns = [projected[0]] + [z_permute(projected[shift], shift) for shift in range(1, 4)]
    own_rows = jnp.concatenate(
        [lax.select_n(z, *[columns[(j - i) % 4] for j in range(4)]) for i in range(4)], axis=-1
    )
    attended = attend(own_rows, key_cache, value_cache, prompt_lengths)
    low_attended, high_attended = attended[: ROWS // 2], attended[ROWS // 2 :]
    low_ring, high_ring = z_ring(low_attended, high_attended)
    blocks = project_out(
        position,
        (low_attended,) + low_ring,
        (high_attended,) + high_ring,
        own_states,
        out_columns,
    )
    came = trade(lambda i: lax.dynamic_index_in_dim(blocks, i, 0, keepdims=False))
    outputs = jnp.stack(
        [block.reshape(4, STEPS, PROMPT_DEV, FEATURES) for block in came], axis=1
    )
    outputs = outputs.transpose(2, 0, 1, 3, 4).reshape(STEPS, 16 * PROMPT_DEV, FEATURES)
    return (
        qkv_updated,
        out_updated,
        qkv_moment_next,
        out_moment_next,
        qkv_second_next,
        out_second_next,
        outputs,
    )


def solution(mesh):
    fine = Mesh(mesh.devices.reshape(SIZES), AXES)
    rows = P(AXES, None)
    caches = P(AXES, None, None, None)
    states = P(None, ("xh", "y"), ("z", "xl", "c"))
    return jax.shard_map(
        on_device,
        mesh=fine,
        in_specs=(rows,) * 8 + (states, caches, caches, P(AXES)),
        out_specs=(rows,) * 6 + (states,),
        check_vma=False,
    )
```

```python
import jax
import jax.numpy as jnp
from jax import lax
from jax.experimental import pallas as pl
from jax.experimental.pallas import tpu as pltpu
from jax.sharding import Mesh
from jax.sharding import PartitionSpec as P

D = 5120
HEADS = 20
KV_HEADS = 4
HEAD_DIM = 128
STEPS = 4
GROUP = HEADS // KV_HEADS
ATT = HEADS * HEAD_DIM
KV = KV_HEADS * HEAD_DIM
QKV = ATT + 2 * KV
PROMPT_DEV = 24
CACHE = 320
ROWS = STEPS * PROMPT_DEV
QKV_COLS = QKV // 4
OUT_COLS = D // 4
FEATURES = D // 16

beta_first = 0.9
beta_second = 0.95
learning_rate = 0.002
weight_decay = 0.1
adam_epsilon = 1e-08
bias_first = 1.0 - 0.9**10
bias_second = 1.0 - 0.95**10
norm_epsilon = 1e-06
rope_base = 1000000.0

SIZES = (2, 4, 4, 2, 2)
AXES = ("xh", "y", "z", "xl", "c")


def adam_update(param, grad, moment, second):
    param_wide = param.astype(jnp.float32)
    grad_wide = grad.astype(jnp.float32)
    moment_next = beta_first * moment + (1.0 - beta_first) * grad_wide
    second_next = beta_second * second + (1.0 - beta_second) * grad_wide * grad_wide
    moment_hat = moment_next / bias_first
    second_hat = second_next / bias_second
    updated = param_wide - learning_rate * (
        moment_hat / (jnp.sqrt(second_hat) + adam_epsilon) + weight_decay * param_wide
    )
    return (updated.astype(jnp.bfloat16), moment_next, second_next)


def device_of(x, y, z, c):
    return ((((x // 2) * 4 + y) * 4 + z) * 2 + x % 2) * 2 + c


def plane_pairs(phase, shift):
    pairs = []
    for x in range(4):
        for y in range(4):
            for z in range(4):
                for c in range(2):
                    if c == phase:
                        target = device_of((x + shift) % 4, y, z, c)
                    else:
                        target = device_of(x, (y + shift) % 4, z, c)
                    pairs.append((device_of(x, y, z, c), target))
    return pairs


def plane_permute(array, phase, shift):
    return lax.ppermute(array, AXES, plane_pairs(phase, shift))


def z_permute(array, shift):
    return lax.ppermute(array, "z", [(j, (j + shift) % 4) for j in range(4)])


def core_permute(array):
    return lax.ppermute(array, "c", [(0, 1), (1, 0)])


def z_ring(low, high):
    low_1, high_3 = z_permute(low, 1), z_permute(high, -1)
    high_1, low_3 = z_permute(high, 1), z_permute(low, -1)
    low_2, high_2 = z_permute(low_1, 1), z_permute(high_3, -1)
    return (low_1, low_2, low_3), (high_1, high_2, high_3)


def plane_gather(block):
    first = jnp.stack(
        [
            block,
            plane_permute(block, 0, 1),
            plane_permute(block, 0, 2),
            plane_permute(block, 0, -1),
        ]
    )
    return (first,) + tuple(plane_permute(first, 1, shift) for shift in (1, 2, -1))


def held_block(held, pos_ref, core_type, x_from, y_from, z_from):
    x_back = (pos_ref[0] - x_from) & 3
    y_back = (pos_ref[1] - y_from) & 3
    z_back = (pos_ref[2] - z_from) & 3
    who = pos_ref[3] ^ core_type
    if core_type == 0:
        block = held[who, y_back, x_back, z_back]
    else:
        block = held[who, x_back, y_back, z_back]
    return block.astype(jnp.float32)


def project_kernel(pos_ref, *refs):
    states_ref, piece_refs, outs = refs[0], refs[1:9], refs[9:13]
    states, held, weight, total, by_shift, sems = refs[13:]
    loads = [
        pltpu.make_async_copy(states_ref.at[block], states.at[block], sems.at[8 + block])
        for block in range(4)
    ]
    loads += [
        pltpu.make_async_copy(piece, held.at[index // 4, index % 4], sems.at[index])
        for index, piece in enumerate(piece_refs)
    ]
    for load in loads:
        load.start()
    for load in loads[:4]:
        load.wait()
    squares = None
    for block in range(4):
        part = states[block].astype(jnp.float32)
        term = jnp.sum(part * part, axis=-1, keepdims=True)
        squares = term if squares is None else squares + term
    factor = lax.rsqrt(squares / D + norm_epsilon)
    for block in range(4):
        part = states[block].astype(jnp.float32)
        states[block] = (part * factor).astype(jnp.bfloat16)
    for load in loads[4:]:
        load.wait()
    z = pos_ref[2]
    for block in range(4):
        for index in range(16 * block, 16 * block + 16):
            d, z_from, xl = index // 8, (index // 2) & 3, index & 1
            x_from, y_from = (d // 4) * 2 + xl, d & 3
            pair = jnp.concatenate(
                [held_block(held, pos_ref, ct, x_from, y_from, z_from) for ct in range(2)], axis=0
            )
            weight[index * 80 : index * 80 + 80, :] = pair.astype(jnp.bfloat16)
        term = jnp.dot(
            states[block],
            weight[block * OUT_COLS : (block + 1) * OUT_COLS, :],
            preferred_element_type=jnp.float32,
        )
        if block == 0:
            total[...] = term
        elif block < 3:
            total[...] += term
        else:
            result = (total[...] + term).astype(jnp.bfloat16)
            for owner in range(4):
                by_shift[(owner - z) & 3] = result[owner * ROWS : (owner + 1) * ROWS]
    for shift in range(4):
        outs[shift][...] = by_shift[shift]


def order_kernel(halves_ref, weight, held, sem):
    copy = pltpu.make_async_copy(halves_ref, held, sem)
    copy.start()
    copy.wait()

    def place(index, carry):
        d, z_from = index // 4, index & 3
        for half in range(2):
            pair = jnp.concatenate(
                [held[d // 4, d & 3, xl, half, z_from].astype(jnp.float32) for xl in range(2)],
                axis=0,
            )
            weight[
                pl.ds(pl.multiple_of(index * 80, 80), 80),
                half * OUT_COLS // 2 : (half + 1) * OUT_COLS // 2,
            ] = pair.astype(jnp.bfloat16)
        return carry

    lax.fori_loop(0, 32, place, 0)


def output_kernel(pos_ref, *refs):
    lows, highs, states, weight, out_ref = refs[:4], refs[4:8], refs[8], refs[9], refs[10]
    z = pos_ref[2]
    for back in range(4):
        owner = (z - back) & 3
        part = jnp.concatenate([lows[back][...], highs[back][...]], axis=0)
        result = jnp.dot(part, weight[...], preferred_element_type=jnp.float32)
        rows = pl.ds(pl.multiple_of(owner * ROWS, ROWS), ROWS)
        result = (states[rows, :].astype(jnp.float32) + result).astype(jnp.bfloat16)
        for block in range(4):
            out_ref[block, owner] = result[:, block * FEATURES : (block + 1) * FEATURES]


SMEM_SPEC = pl.BlockSpec(memory_space=pltpu.SMEM)
VMEM_SPEC = pl.BlockSpec(memory_space=pltpu.VMEM)
ANY_SPEC = pl.BlockSpec(memory_space=pl.ANY)


def bf16(*shape):
    return jax.ShapeDtypeStruct(shape, jnp.bfloat16)


def params(mebibytes):
    return pltpu.CompilerParams(vmem_limit_bytes=mebibytes * 1024 * 1024)


def cost(flops, size):
    return pl.CostEstimate(flops=flops, bytes_accessed=size, transcendentals=0)


def project(position, states, pieces):
    return pl.pallas_call(
        project_kernel,
        out_shape=[bf16(ROWS, QKV_COLS)] * 4,
        in_specs=[SMEM_SPEC] + [ANY_SPEC] * 9,
        out_specs=[VMEM_SPEC] * 4,
        scratch_shapes=[
            pltpu.VMEM((4, 4 * ROWS, OUT_COLS), jnp.bfloat16),
            pltpu.VMEM((2, 4, 4, 4, 40, QKV_COLS), jnp.bfloat16),
            pltpu.VMEM((D, QKV_COLS), jnp.bfloat16),
            pltpu.VMEM((4 * ROWS, QKV_COLS), jnp.float32),
            pltpu.VMEM((4, ROWS, QKV_COLS), jnp.bfloat16),
            pltpu.SemaphoreType.DMA((12,)),
        ],
        compiler_params=params(58),
        cost_estimate=cost(8 * ROWS * D * QKV_COLS, 20000000),
    )(position, states, *pieces)


def order(halves):
    return pl.pallas_call(
        order_kernel,
        out_shape=bf16(ATT, OUT_COLS),
        in_specs=[ANY_SPEC],
        out_specs=VMEM_SPEC,
        scratch_shapes=[
            pltpu.VMEM(halves.shape, jnp.bfloat16),
            pltpu.SemaphoreType.DMA(()),
        ],
        compiler_params=params(24),
        cost_estimate=cost(0, 14000000),
    )(halves)


def project_out(position, lows, highs, states, weight):
    return pl.pallas_call(
        output_kernel,
        out_shape=bf16(4, 4, ROWS, FEATURES),
        in_specs=[SMEM_SPEC] + [VMEM_SPEC] * 10,
        out_specs=VMEM_SPEC,
        compiler_params=params(24),
        cost_estimate=cost(8 * ROWS * ATT * OUT_COLS, 12000000),
    )(position, *lows, *highs, states, weight)


def stack_kernel(*refs):
    for index in range(4):
        refs[5][index] = refs[index][:, :QKV_COLS]
        refs[6][index] = refs[index][:, QKV_COLS:]


def stack_blocks(blocks, states):
    return pl.pallas_call(
        stack_kernel,
        out_shape=[
            bf16(4, 40, QKV_COLS),
            bf16(4, 40, OUT_COLS // 2),
            jax.ShapeDtypeStruct(states.shape, states.dtype),
        ],
        in_specs=[VMEM_SPEC] * 4 + [ANY_SPEC],
        out_specs=[VMEM_SPEC] * 2 + [ANY_SPEC],
        input_output_aliases={4: 2},
    )(*blocks, states)


def halves_kernel(pos_ref, block_ref, *refs):
    c = pos_ref[3]
    for index in range(4):
        from_block = block_ref[(pos_ref[2] - index) & 3].astype(jnp.float32)
        low, high = from_block[:20], from_block[20:]
        refs[-2][index] = jnp.where(c == 0, low, high).astype(jnp.bfloat16)
        refs[-1][index] = jnp.where(c == 0, high, low).astype(jnp.bfloat16)


def halves_of(position, block, *after):
    return pl.pallas_call(
        halves_kernel,
        out_shape=[bf16(4, 20, OUT_COLS // 2)] * 2,
        in_specs=[SMEM_SPEC, VMEM_SPEC] + [ANY_SPEC] * len(after),
        out_specs=[VMEM_SPEC] * 2,
    )(position, block, *after)


PAIRS = PROMPT_DEV // 2
STEP_PROMPTS = 8
TALL = 2 * STEPS * GROUP


def spread_rows(pos_ref, columns, cosine, sine_part, by_z, heads, queries, keys, values):
    z = pos_ref[2]
    for back in range(4):
        by_z[(z - back) & 3] = columns[back][...]
    for head in range(HEADS + 2 * KV_HEADS):
        lane = (head % 7) * HEAD_DIM
        widened = by_z[head // 7, :, lane : lane + HEAD_DIM].astype(jnp.float32)
        if head < HEADS + KV_HEADS:
            widened = widened * cosine[...] + pltpu.roll(widened, HEAD_DIM // 2, 1) * sine_part[...]
            widened = widened.astype(jnp.bfloat16).astype(jnp.float32)
        heads[head] = widened
    for prompt in range(PROMPT_DEV):
        pair, place = prompt // 2, (prompt % 2) * STEPS
        rows = pl.ds(prompt, STEPS, stride=PROMPT_DEV)
        for head in range(HEADS):
            start = (head % GROUP) * 2 * STEPS + place
            queries[pair, head // GROUP, start : start + STEPS, :] = heads[head, rows, :]
        for group in range(KV_HEADS):
            span = slice(place, place + STEPS)
            keys[pair, group, span, :] = heads[HEADS + group, rows, :]
            values[pair, group, span, :] = heads[HEADS + KV_HEADS + group, rows, :]


def attend_kernel(pos_ref, length_ref, *refs):
    columns, cosine, sine_part = refs[:4], refs[4], refs[5]
    key_ref, value_ref, low_ref, high_ref = refs[6:10]
    by_z, heads, queries, keys, values = refs[10:]
    step = pl.program_id(0)

    @pl.when(step == 0)
    def _():
        spread_rows(pos_ref, columns, cosine, sine_part, by_z, heads, queries, keys, values)

    score_scale = HEAD_DIM ** (-0.5)
    by_last = (((1,), (1,)), ((), ()))
    row = lax.broadcasted_iota(jnp.int32, (TALL, 1), 0)
    second = ((row >> 2) & 1) == 1
    fresh_column = lax.broadcasted_iota(jnp.int32, (TALL, 2 * STEPS), 1)
    fresh_mask = ((fresh_column >> 2) == ((row >> 2) & 1)) & ((fresh_column & 3) <= (row & 3))
    column = lax.broadcasted_iota(jnp.int32, (TALL, CACHE), 1)
    places = [(i, group) for i in range(STEP_PROMPTS // 2) for group in range(KV_HEADS)]
    first = step * (STEP_PROMPTS // 2)
    masks = []
    for inner in range(STEP_PROMPTS // 2):
        pair = first + inner
        length = jnp.where(second, length_ref[2 * pair + 1], length_ref[2 * pair])
        masks.append(column < length)
    tiles = [
        tuple(part[first + i, group].astype(jnp.bfloat16) for part in (queries, keys, values))
        for i, group in places
    ]

    def scores(query, key):
        return lax.dot_general(query, key, by_last, preferred_element_type=jnp.float32)

    def weighted(weights, rows):
        return jnp.dot(weights, rows, preferred_element_type=jnp.float32)

    cache_scores = [
        jnp.where(
            second,
            scores(query, key_ref[2 * i + 1, group]),
            scores(query, key_ref[2 * i, group]),
        )
        for (i, group), (query, _, _) in zip(places, tiles)
    ]
    fresh_scores = [scores(query, key) for query, key, _ in tiles]
    cache_scores = [
        jnp.where(masks[i], part * score_scale, -1e30)
        for (i, _), part in zip(places, cache_scores)
    ]
    fresh_scores = [jnp.where(fresh_mask, part * score_scale, -1e30) for part in fresh_scores]
    largest = [
        jnp.maximum(jnp.max(a, axis=-1, keepdims=True), jnp.max(b, axis=-1, keepdims=True))
        for a, b in zip(cache_scores, fresh_scores)
    ]
    cache_exp = [jnp.exp(part - top) for part, top in zip(cache_scores, largest)]
    fresh_exp = [jnp.exp(part - top) for part, top in zip(fresh_scores, largest)]
    denominator = [
        jnp.sum(a, axis=-1, keepdims=True) + jnp.sum(b, axis=-1, keepdims=True)
        for a, b in zip(cache_exp, fresh_exp)
    ]
    cache_weights = [(a / total).astype(jnp.bfloat16) for a, total in zip(cache_exp, denominator)]
    fresh_weights = [(b / total).astype(jnp.bfloat16) for b, total in zip(fresh_exp, denominator)]
    results = [
        jnp.where(
            second,
            weighted(weights, value_ref[2 * i + 1, group]),
            weighted(weights, value_ref[2 * i, group]),
        )
        + weighted(fresh, tile[2])
        for (i, group), weights, fresh, tile in zip(places, cache_weights, fresh_weights, tiles)
    ]
    for (i, group), result in zip(places, results):
        queries[first + i, group] = result

    @pl.when(step == pl.num_programs(0) - 1)
    def _():
        for prompt in range(PROMPT_DEV):
            rows = pl.ds(prompt, STEPS, stride=PROMPT_DEV)
            for head in range(HEADS):
                start = (head % GROUP) * 2 * STEPS + (prompt % 2) * STEPS
                heads[head, rows, :] = queries[
                    prompt // 2, head // GROUP, start : start + STEPS, :
                ]
        for head in range(HEADS):
            lane = head * HEAD_DIM
            result = heads[head].astype(jnp.bfloat16)
            low_ref[:, lane : lane + HEAD_DIM] = result[: ROWS // 2]
            high_ref[:, lane : lane + HEAD_DIM] = result[ROWS // 2 :]


def attend(position, columns, key_cache, value_cache, lengths):
    half_dim = HEAD_DIM // 2
    frequencies = rope_base ** (-2.0 * jnp.arange(half_dim, dtype=jnp.float32) / HEAD_DIM)
    positions = lengths[None, :] + jnp.arange(STEPS, dtype=jnp.int32)[:, None]
    angles = positions.reshape(ROWS).astype(jnp.float32)[:, None] * frequencies[None, :]
    cosine, sine_part = jnp.cos(angles), jnp.sin(angles)
    cache_spec = pl.BlockSpec(
        (STEP_PROMPTS, KV_HEADS, CACHE, HEAD_DIM), lambda step: (step, 0, 0, 0)
    )
    pair_shape = (PAIRS, KV_HEADS, 2 * STEPS, HEAD_DIM)
    return pl.pallas_call(
        attend_kernel,
        grid=(PROMPT_DEV // STEP_PROMPTS,),
        out_shape=[bf16(ROWS // 2, ATT)] * 2,
        in_specs=[SMEM_SPEC] * 2 + [VMEM_SPEC] * 6 + [cache_spec] * 2,
        out_specs=[pl.BlockSpec((ROWS // 2, ATT), lambda step: (0, 0))] * 2,
        scratch_shapes=[
            pltpu.VMEM((4, ROWS, QKV_COLS), jnp.bfloat16),
            pltpu.VMEM((HEADS + 2 * KV_HEADS, ROWS, HEAD_DIM), jnp.float32),
            pltpu.VMEM((PAIRS, KV_HEADS, TALL, HEAD_DIM), jnp.float32),
            pltpu.VMEM(pair_shape, jnp.float32),
            pltpu.VMEM(pair_shape, jnp.float32),
        ],
        compiler_params=params(58),
        cost_estimate=cost(4 * ROWS * HEADS * HEAD_DIM * CACHE, 17000000),
    )(
        position,
        lengths,
        *columns,
        jnp.concatenate([cosine, cosine], axis=-1),
        jnp.concatenate([-sine_part, sine_part], axis=-1),
        key_cache,
        value_cache,
    )


def on_device(
    qkv_weight,
    out_weight,
    qkv_grad,
    out_grad,
    qkv_moment,
    out_moment,
    qkv_second,
    out_second,
    step_states,
    key_cache,
    value_cache,
    prompt_lengths,
):
    xh, y, z, xl, c = (lax.axis_index(axis) for axis in AXES)
    place = xl * 2 + c
    position = jnp.stack([xh * 2 + xl, y, z, c]).astype(jnp.int32)

    def trade(block_to):
        came = [block_to(place)]
        for other in range(1, 4):
            came.append(
                lax.ppermute(
                    block_to(place ^ other), ("xl", "c"), [(i, i ^ other) for i in range(4)]
                )
            )
        return [lax.select_n(place, *[came[i ^ j] for j in range(4)]) for i in range(4)]

    qkv_updated, qkv_moment_next, qkv_second_next = adam_update(
        qkv_weight, qkv_grad, qkv_moment, qkv_second
    )
    out_updated, out_moment_next, out_second_next = adam_update(
        out_weight, out_grad, out_moment, out_second
    )

    by_place = step_states.reshape(STEPS, 4, 4, PROMPT_DEV, FEATURES)
    by_place = by_place.transpose(2, 1, 0, 3, 4).reshape(4, 4 * ROWS, FEATURES)
    came = trade(lambda i: lax.dynamic_index_in_dim(by_place, i, 0, keepdims=False))
    own_states = jnp.concatenate(came, axis=-1)

    by_z = jnp.concatenate(
        [
            qkv_updated.reshape(40, 4, QKV_COLS).transpose(1, 0, 2),
            out_updated.reshape(20, 4, 2, OUT_COLS // 2)
            .transpose(1, 2, 0, 3)
            .reshape(4, 40, OUT_COLS // 2),
        ],
        axis=-1,
    )
    blocks = [lax.dynamic_index_in_dim(by_z, z, 0, keepdims=False)] + [
        z_permute(lax.dynamic_index_in_dim(by_z, (z + shift) & 3, 0, keepdims=False), shift)
        for shift in range(1, 4)
    ]
    qkv_block, out_block, own_states = stack_blocks(blocks, own_states)
    all_states = lax.all_gather(own_states, "z")
    qkv_pieces = plane_gather(qkv_block)
    qkv_pieces = qkv_pieces + tuple(core_permute(piece) for piece in qkv_pieces)
    projected = project(position, all_states, qkv_pieces)

    own_half, sent_half = halves_of(position, out_block, *qkv_pieces[1:4])
    other_half = core_permute(sent_half)
    both = jnp.where(
        c == 0,
        jnp.concatenate([own_half, other_half], axis=1),
        jnp.concatenate([other_half, own_half], axis=1),
    )
    gathered = lax.all_gather(both, ("xh", "y", "xl", "c"))
    out_columns = order(gathered.reshape(2, 4, 2, 2, 4, 40, OUT_COLS // 2))

    columns = [projected[0]] + [z_permute(projected[shift], shift) for shift in range(1, 4)]
    low_attended, high_attended = attend(
        position, columns, key_cache, value_cache, prompt_lengths
    )
    low_ring, high_ring = z_ring(low_attended, high_attended)
    blocks = project_out(
        position,
        (low_attended,) + low_ring,
        (high_attended,) + high_ring,
        own_states,
        out_columns,
    )
    came = trade(lambda i: lax.dynamic_index_in_dim(blocks, i, 0, keepdims=False))
    outputs = jnp.stack(
        [block.reshape(4, STEPS, PROMPT_DEV, FEATURES) for block in came], axis=1
    )
    outputs = outputs.transpose(2, 0, 1, 3, 4).reshape(STEPS, 16 * PROMPT_DEV, FEATURES)
    return (
        qkv_updated,
        out_updated,
        qkv_moment_next,
        out_moment_next,
        qkv_second_next,
        out_second_next,
        outputs,
    )


def solution(mesh):
    fine = Mesh(mesh.devices.reshape(SIZES), AXES)
    rows = P(AXES, None)
    caches = P(AXES, None, None, None)
    states = P(None, ("xh", "y"), ("z", "xl", "c"))
    return jax.shard_map(
        on_device,
        mesh=fine,
        in_specs=(rows,) * 8 + (states, caches, caches, P(AXES)),
        out_specs=(rows,) * 6 + (states,),
        check_vma=False,
    )
```

```python
import functools

import jax
import jax.numpy as jnp
from jax import lax
from jax.experimental import pallas as pl
from jax.experimental.pallas import tpu as pltpu
from jax.sharding import Mesh
from jax.sharding import PartitionSpec as P

D = 5120
HEADS = 20
KV_HEADS = 4
HEAD_DIM = 128
STEPS = 4
GROUP = HEADS // KV_HEADS
ATT = HEADS * HEAD_DIM
KV = KV_HEADS * HEAD_DIM
QKV = ATT + 2 * KV
PROMPT_DEV = 24
CACHE = 320
ROWS = STEPS * PROMPT_DEV
QKV_COLS = QKV // 4
OUT_COLS = D // 4
FEATURES = D // 16

beta_first = 0.9
beta_second = 0.95
learning_rate = 0.002
weight_decay = 0.1
adam_epsilon = 1e-08
bias_first = 1.0 - 0.9**10
bias_second = 1.0 - 0.95**10
norm_epsilon = 1e-06
rope_base = 1000000.0

SIZES = (2, 4, 4, 2, 2)
AXES = ("xh", "y", "z", "xl", "c")


def adam_update(param, grad, moment, second):
    param_wide = param.astype(jnp.float32)
    grad_wide = grad.astype(jnp.float32)
    moment_next = beta_first * moment + (1.0 - beta_first) * grad_wide
    second_next = beta_second * second + (1.0 - beta_second) * grad_wide * grad_wide
    moment_hat = moment_next / bias_first
    second_hat = second_next / bias_second
    updated = param_wide - learning_rate * (
        moment_hat / (jnp.sqrt(second_hat) + adam_epsilon) + weight_decay * param_wide
    )
    return (updated.astype(jnp.bfloat16), moment_next, second_next)


def device_of(x, y, z, c):
    return ((((x // 2) * 4 + y) * 4 + z) * 2 + x % 2) * 2 + c


def plane_pairs(phase, shift):
    pairs = []
    for x in range(4):
        for y in range(4):
            for z in range(4):
                for c in range(2):
                    if c == phase:
                        target = device_of((x + shift) % 4, y, z, c)
                    else:
                        target = device_of(x, (y + shift) % 4, z, c)
                    pairs.append((device_of(x, y, z, c), target))
    return pairs


def plane_permute(array, phase, shift):
    return lax.ppermute(array, AXES, plane_pairs(phase, shift))


def z_permute(array, shift):
    return lax.ppermute(array, "z", [(j, (j + shift) % 4) for j in range(4)])


def core_permute(array):
    return lax.ppermute(array, "c", [(0, 1), (1, 0)])


def z_ring(low, high):
    low_1, high_3 = z_permute(low, 1), z_permute(high, -1)
    high_1, low_3 = z_permute(high, 1), z_permute(low, -1)
    low_2, high_2 = z_permute(low_1, 1), z_permute(high_3, -1)
    return (low_1, low_2, low_3), (high_1, high_2, high_3)


def plane_gather(block):
    first = jnp.stack(
        [
            block,
            plane_permute(block, 0, 1),
            plane_permute(block, 0, 2),
            plane_permute(block, 0, -1),
        ]
    )
    return (first,) + tuple(plane_permute(first, 1, shift) for shift in (1, 2, -1))


def held_block(held, pos_ref, core_type, x_from, y_from, z_from):
    x_back = (pos_ref[0] - x_from) & 3
    y_back = (pos_ref[1] - y_from) & 3
    z_back = (pos_ref[2] - z_from) & 3
    who = pos_ref[3] ^ core_type
    if core_type == 0:
        block = held[who, y_back, x_back, z_back]
    else:
        block = held[who, x_back, y_back, z_back]
    return block.astype(jnp.float32)


def project_kernel(pos_ref, *refs):
    states_ref, piece_refs, outs = refs[0], refs[1:9], refs[9:13]
    states, held, weight, total, by_shift, sems = refs[13:]
    loads = [
        pltpu.make_async_copy(states_ref.at[block], states.at[block], sems.at[8 + block])
        for block in range(4)
    ]
    loads += [
        pltpu.make_async_copy(piece, held.at[index // 4, index % 4], sems.at[index])
        for index, piece in enumerate(piece_refs)
    ]
    for load in loads:
        load.start()
    for load in loads[:4]:
        load.wait()
    squares = None
    for block in range(4):
        part = states[block].astype(jnp.float32)
        term = jnp.sum(part * part, axis=-1, keepdims=True)
        squares = term if squares is None else squares + term
    factor = lax.rsqrt(squares / D + norm_epsilon)
    for block in range(4):
        part = states[block].astype(jnp.float32)
        states[block] = (part * factor).astype(jnp.bfloat16)
    for load in loads[4:]:
        load.wait()
    z = pos_ref[2]
    for block in range(4):
        for index in range(16 * block, 16 * block + 16):
            d, z_from, xl = index // 8, (index // 2) & 3, index & 1
            x_from, y_from = (d // 4) * 2 + xl, d & 3
            pair = jnp.concatenate(
                [held_block(held, pos_ref, ct, x_from, y_from, z_from) for ct in range(2)], axis=0
            )
            weight[index * 80 : index * 80 + 80, :] = pair.astype(jnp.bfloat16)
        term = jnp.dot(
            states[block],
            weight[block * OUT_COLS : (block + 1) * OUT_COLS, :],
            preferred_element_type=jnp.float32,
        )
        if block == 0:
            total[...] = term
        elif block < 3:
            total[...] += term
        else:
            result = (total[...] + term).astype(jnp.bfloat16)
            for owner in range(4):
                by_shift[(owner - z) & 3] = result[owner * ROWS : (owner + 1) * ROWS]
    for shift in range(4):
        outs[shift][...] = by_shift[shift]


def order_kernel(halves_ref, weight, held, sem):
    copy = pltpu.make_async_copy(halves_ref, held, sem)
    copy.start()
    copy.wait()

    def place(index, carry):
        d, z_from = index // 4, index & 3
        for half in range(2):
            pair = jnp.concatenate(
                [held[d // 4, d & 3, xl, half, z_from].astype(jnp.float32) for xl in range(2)],
                axis=0,
            )
            weight[
                pl.ds(pl.multiple_of(index * 80, 80), 80),
                half * OUT_COLS // 2 : (half + 1) * OUT_COLS // 2,
            ] = pair.astype(jnp.bfloat16)
        return carry

    lax.fori_loop(0, 32, place, 0)


def output_kernel(flip, pos_ref, *refs):
    lows, highs, states, weight, out_ref = refs[:4], refs[4:8], refs[8], refs[9], refs[-1]
    z = pos_ref[2]
    side = (pos_ref[0] & 1) ^ flip
    lanes = pl.ds(pl.multiple_of(side * 2 * FEATURES, 2 * FEATURES), 2 * FEATURES)
    for back in range(4):
        owner = (z - back) & 3
        part = jnp.concatenate([lows[back][...], highs[back][...]], axis=0)
        result = jnp.dot(part, weight[:, lanes], preferred_element_type=jnp.float32)
        rows = pl.ds(pl.multiple_of(owner * ROWS, ROWS), ROWS)
        result = (states[rows, lanes].astype(jnp.float32) + result).astype(jnp.bfloat16)
        for core in range(2):
            out_ref[core, owner] = result[:, core * FEATURES : (core + 1) * FEATURES]


SMEM_SPEC = pl.BlockSpec(memory_space=pltpu.SMEM)
VMEM_SPEC = pl.BlockSpec(memory_space=pltpu.VMEM)
ANY_SPEC = pl.BlockSpec(memory_space=pl.ANY)


def bf16(*shape):
    return jax.ShapeDtypeStruct(shape, jnp.bfloat16)


def params(mebibytes):
    return pltpu.CompilerParams(vmem_limit_bytes=mebibytes * 1024 * 1024)


def cost(flops, size):
    return pl.CostEstimate(flops=flops, bytes_accessed=size, transcendentals=0)


def project(position, states, pieces):
    return pl.pallas_call(
        project_kernel,
        out_shape=[bf16(ROWS, QKV_COLS)] * 4,
        in_specs=[SMEM_SPEC] + [ANY_SPEC] * 9,
        out_specs=[VMEM_SPEC] * 4,
        scratch_shapes=[
            pltpu.VMEM((4, 4 * ROWS, OUT_COLS), jnp.bfloat16),
            pltpu.VMEM((2, 4, 4, 4, 40, QKV_COLS), jnp.bfloat16),
            pltpu.VMEM((D, QKV_COLS), jnp.bfloat16),
            pltpu.VMEM((4 * ROWS, QKV_COLS), jnp.float32),
            pltpu.VMEM((4, ROWS, QKV_COLS), jnp.bfloat16),
            pltpu.SemaphoreType.DMA((12,)),
        ],
        compiler_params=params(58),
        cost_estimate=cost(8 * ROWS * D * QKV_COLS, 20000000),
    )(position, states, *pieces)


def order(halves):
    return pl.pallas_call(
        order_kernel,
        out_shape=bf16(ATT, OUT_COLS),
        in_specs=[ANY_SPEC],
        out_specs=VMEM_SPEC,
        scratch_shapes=[
            pltpu.VMEM(halves.shape, jnp.bfloat16),
            pltpu.SemaphoreType.DMA(()),
        ],
        compiler_params=params(24),
        cost_estimate=cost(0, 14000000),
    )(halves)


def project_out(flip, position, lows, highs, states, weight, *after):
    return pl.pallas_call(
        functools.partial(output_kernel, flip),
        out_shape=bf16(2, 4, ROWS, FEATURES),
        in_specs=[SMEM_SPEC] + [VMEM_SPEC] * 10 + [ANY_SPEC] * len(after),
        out_specs=VMEM_SPEC,
        compiler_params=params(24),
        cost_estimate=cost(4 * ROWS * ATT * OUT_COLS, 8000000),
    )(position, *lows, *highs, states, weight, *after)


def stack_kernel(*refs):
    for index in range(4):
        refs[5][index] = refs[index][:, :QKV_COLS]
        refs[6][index] = refs[index][:, QKV_COLS:]


def stack_blocks(blocks, states):
    return pl.pallas_call(
        stack_kernel,
        out_shape=[
            bf16(4, 40, QKV_COLS),
            bf16(4, 40, OUT_COLS // 2),
            jax.ShapeDtypeStruct(states.shape, states.dtype),
        ],
        in_specs=[VMEM_SPEC] * 4 + [ANY_SPEC],
        out_specs=[VMEM_SPEC] * 2 + [ANY_SPEC],
        input_output_aliases={4: 2},
    )(*blocks, states)


def halves_kernel(pos_ref, block_ref, *refs):
    c = pos_ref[3]
    for index in range(4):
        from_block = block_ref[(pos_ref[2] - index) & 3].astype(jnp.float32)
        low, high = from_block[:20], from_block[20:]
        refs[-2][index] = jnp.where(c == 0, low, high).astype(jnp.bfloat16)
        refs[-1][index] = jnp.where(c == 0, high, low).astype(jnp.bfloat16)


def halves_of(position, block, *after):
    return pl.pallas_call(
        halves_kernel,
        out_shape=[bf16(4, 20, OUT_COLS // 2)] * 2,
        in_specs=[SMEM_SPEC, VMEM_SPEC] + [ANY_SPEC] * len(after),
        out_specs=[VMEM_SPEC] * 2,
    )(position, block, *after)


PAIRS = PROMPT_DEV // 2
STEP_PROMPTS = 8
TALL = 2 * STEPS * GROUP


def spread_rows(pos_ref, columns, cosine, sine_part, by_z, heads, queries, keys, values):
    z = pos_ref[2]
    for back in range(4):
        by_z[(z - back) & 3] = columns[back][...]
    for head in range(HEADS + 2 * KV_HEADS):
        lane = (head % 7) * HEAD_DIM
        widened = by_z[head // 7, :, lane : lane + HEAD_DIM].astype(jnp.float32)
        if head < HEADS + KV_HEADS:
            widened = widened * cosine[...] + pltpu.roll(widened, HEAD_DIM // 2, 1) * sine_part[...]
            widened = widened.astype(jnp.bfloat16).astype(jnp.float32)
        heads[head] = widened
    for prompt in range(PROMPT_DEV):
        pair, place = prompt // 2, (prompt % 2) * STEPS
        rows = pl.ds(prompt, STEPS, stride=PROMPT_DEV)
        for head in range(HEADS):
            start = (head % GROUP) * 2 * STEPS + place
            queries[pair, head // GROUP, start : start + STEPS, :] = heads[head, rows, :]
        for group in range(KV_HEADS):
            span = slice(place, place + STEPS)
            keys[pair, group, span, :] = heads[HEADS + group, rows, :]
            values[pair, group, span, :] = heads[HEADS + KV_HEADS + group, rows, :]


def attend_kernel(pos_ref, length_ref, *refs):
    columns, cosine, sine_part = refs[:4], refs[4], refs[5]
    key_ref, value_ref, low_ref, high_ref = refs[6:10]
    by_z, heads, queries, keys, values = refs[10:]
    step = pl.program_id(0)

    @pl.when(step == 0)
    def _():
        spread_rows(pos_ref, columns, cosine, sine_part, by_z, heads, queries, keys, values)

    score_scale = HEAD_DIM ** (-0.5)
    by_last = (((1,), (1,)), ((), ()))
    row = lax.broadcasted_iota(jnp.int32, (TALL, 1), 0)
    second = ((row >> 2) & 1) == 1
    fresh_column = lax.broadcasted_iota(jnp.int32, (TALL, 2 * STEPS), 1)
    fresh_mask = ((fresh_column >> 2) == ((row >> 2) & 1)) & ((fresh_column & 3) <= (row & 3))
    column = lax.broadcasted_iota(jnp.int32, (TALL, CACHE), 1)
    places = [(i, group) for i in range(STEP_PROMPTS // 2) for group in range(KV_HEADS)]
    first = step * (STEP_PROMPTS // 2)
    masks = []
    for inner in range(STEP_PROMPTS // 2):
        pair = first + inner
        length = jnp.where(second, length_ref[2 * pair + 1], length_ref[2 * pair])
        masks.append(column < length)
    tiles = [
        tuple(part[first + i, group].astype(jnp.bfloat16) for part in (queries, keys, values))
        for i, group in places
    ]

    def scores(query, key):
        return lax.dot_general(query, key, by_last, preferred_element_type=jnp.float32)

    def weighted(weights, rows):
        return jnp.dot(weights, rows, preferred_element_type=jnp.float32)

    cache_scores = [
        jnp.where(
            second,
            scores(query, key_ref[2 * i + 1, group]),
            scores(query, key_ref[2 * i, group]),
        )
        for (i, group), (query, _, _) in zip(places, tiles)
    ]
    fresh_scores = [scores(query, key) for query, key, _ in tiles]
    cache_scores = [
        jnp.where(masks[i], part * score_scale, -1e30)
        for (i, _), part in zip(places, cache_scores)
    ]
    fresh_scores = [jnp.where(fresh_mask, part * score_scale, -1e30) for part in fresh_scores]
    largest = [
        jnp.maximum(jnp.max(a, axis=-1, keepdims=True), jnp.max(b, axis=-1, keepdims=True))
        for a, b in zip(cache_scores, fresh_scores)
    ]
    cache_exp = [jnp.exp(part - top) for part, top in zip(cache_scores, largest)]
    fresh_exp = [jnp.exp(part - top) for part, top in zip(fresh_scores, largest)]
    denominator = [
        jnp.sum(a, axis=-1, keepdims=True) + jnp.sum(b, axis=-1, keepdims=True)
        for a, b in zip(cache_exp, fresh_exp)
    ]
    cache_weights = [(a / total).astype(jnp.bfloat16) for a, total in zip(cache_exp, denominator)]
    fresh_weights = [(b / total).astype(jnp.bfloat16) for b, total in zip(fresh_exp, denominator)]
    results = [
        jnp.where(
            second,
            weighted(weights, value_ref[2 * i + 1, group]),
            weighted(weights, value_ref[2 * i, group]),
        )
        + weighted(fresh, tile[2])
        for (i, group), weights, fresh, tile in zip(places, cache_weights, fresh_weights, tiles)
    ]
    for (i, group), result in zip(places, results):
        queries[first + i, group] = result

    @pl.when(step == pl.num_programs(0) - 1)
    def _():
        for prompt in range(PROMPT_DEV):
            rows = pl.ds(prompt, STEPS, stride=PROMPT_DEV)
            for head in range(HEADS):
                start = (head % GROUP) * 2 * STEPS + (prompt % 2) * STEPS
                heads[head, rows, :] = queries[
                    prompt // 2, head // GROUP, start : start + STEPS, :
                ]
        for head in range(HEADS):
            lane = head * HEAD_DIM
            result = heads[head].astype(jnp.bfloat16)
            low_ref[:, lane : lane + HEAD_DIM] = result[: ROWS // 2]
            high_ref[:, lane : lane + HEAD_DIM] = result[ROWS // 2 :]


def attend(position, columns, key_cache, value_cache, lengths):
    half_dim = HEAD_DIM // 2
    frequencies = rope_base ** (-2.0 * jnp.arange(half_dim, dtype=jnp.float32) / HEAD_DIM)
    positions = lengths[None, :] + jnp.arange(STEPS, dtype=jnp.int32)[:, None]
    angles = positions.reshape(ROWS).astype(jnp.float32)[:, None] * frequencies[None, :]
    cosine, sine_part = jnp.cos(angles), jnp.sin(angles)
    cache_spec = pl.BlockSpec(
        (STEP_PROMPTS, KV_HEADS, CACHE, HEAD_DIM), lambda step: (step, 0, 0, 0)
    )
    pair_shape = (PAIRS, KV_HEADS, 2 * STEPS, HEAD_DIM)
    return pl.pallas_call(
        attend_kernel,
        grid=(PROMPT_DEV // STEP_PROMPTS,),
        out_shape=[bf16(ROWS // 2, ATT)] * 2,
        in_specs=[SMEM_SPEC] * 2 + [VMEM_SPEC] * 6 + [cache_spec] * 2,
        out_specs=[pl.BlockSpec((ROWS // 2, ATT), lambda step: (0, 0))] * 2,
        scratch_shapes=[
            pltpu.VMEM((4, ROWS, QKV_COLS), jnp.bfloat16),
            pltpu.VMEM((HEADS + 2 * KV_HEADS, ROWS, HEAD_DIM), jnp.float32),
            pltpu.VMEM((PAIRS, KV_HEADS, TALL, HEAD_DIM), jnp.float32),
            pltpu.VMEM(pair_shape, jnp.float32),
            pltpu.VMEM(pair_shape, jnp.float32),
        ],
        compiler_params=params(58),
        cost_estimate=cost(4 * ROWS * HEADS * HEAD_DIM * CACHE, 17000000),
    )(
        position,
        lengths,
        *columns,
        jnp.concatenate([cosine, cosine], axis=-1),
        jnp.concatenate([-sine_part, sine_part], axis=-1),
        key_cache,
        value_cache,
    )


def on_device(
    qkv_weight,
    out_weight,
    qkv_grad,
    out_grad,
    qkv_moment,
    out_moment,
    qkv_second,
    out_second,
    step_states,
    key_cache,
    value_cache,
    prompt_lengths,
):
    xh, y, z, xl, c = (lax.axis_index(axis) for axis in AXES)
    place = xl * 2 + c
    position = jnp.stack([xh * 2 + xl, y, z, c]).astype(jnp.int32)

    def trade(block_for):
        came = [block_for(0)]
        for other in range(1, 4):
            came.append(
                lax.ppermute(block_for(other), ("xl", "c"), [(i, i ^ other) for i in range(4)])
            )
        return [lax.select_n(place, *[came[i ^ j] for j in range(4)]) for i in range(4)]

    qkv_updated, qkv_moment_next, qkv_second_next = adam_update(
        qkv_weight, qkv_grad, qkv_moment, qkv_second
    )
    out_updated, out_moment_next, out_second_next = adam_update(
        out_weight, out_grad, out_moment, out_second
    )

    by_place = step_states.reshape(STEPS, 4, 4, PROMPT_DEV, FEATURES)
    by_place = by_place.transpose(2, 1, 0, 3, 4).reshape(4, 4 * ROWS, FEATURES)
    came = trade(
        lambda other: lax.dynamic_index_in_dim(by_place, place ^ other, 0, keepdims=False)
    )
    own_states = jnp.concatenate(came, axis=-1)

    by_z = jnp.concatenate(
        [
            qkv_updated.reshape(40, 4, QKV_COLS).transpose(1, 0, 2),
            out_updated.reshape(20, 4, 2, OUT_COLS // 2)
            .transpose(1, 2, 0, 3)
            .reshape(4, 40, OUT_COLS // 2),
        ],
        axis=-1,
    )
    blocks = [lax.dynamic_index_in_dim(by_z, z, 0, keepdims=False)] + [
        z_permute(lax.dynamic_index_in_dim(by_z, (z + shift) & 3, 0, keepdims=False), shift)
        for shift in range(1, 4)
    ]
    qkv_block, out_block, own_states = stack_blocks(blocks, own_states)
    all_states = lax.all_gather(own_states, "z")
    qkv_pieces = plane_gather(qkv_block)
    qkv_pieces = qkv_pieces + tuple(core_permute(piece) for piece in qkv_pieces)
    projected = project(position, all_states, qkv_pieces)

    own_half, sent_half = halves_of(position, out_block, *qkv_pieces[1:4])
    other_half = core_permute(sent_half)
    both = jnp.where(
        c == 0,
        jnp.concatenate([own_half, other_half], axis=1),
        jnp.concatenate([other_half, own_half], axis=1),
    )
    gathered = lax.all_gather(both, ("xh", "y", "xl", "c"))
    out_columns = order(gathered.reshape(2, 4, 2, 2, 4, 40, OUT_COLS // 2))

    columns = [projected[0]] + [z_permute(projected[shift], shift) for shift in range(1, 4)]
    low_attended, high_attended = attend(
        position, columns, key_cache, value_cache, prompt_lengths
    )
    low_ring, high_ring = z_ring(low_attended, high_attended)
    operands = (
        position,
        (low_attended,) + low_ring,
        (high_attended,) + high_ring,
        own_states,
        out_columns,
    )
    far_blocks = project_out(1, *operands)

    def send(blocks, other):
        block = lax.dynamic_index_in_dim(blocks, c ^ (other & 1), 0, keepdims=False)
        return lax.ppermute(block, ("xl", "c"), [(i, i ^ other) for i in range(4)])

    from_far = [send(far_blocks, other) for other in (2, 3)]
    near_blocks = project_out(0, *operands, from_far[1])
    own_block = lax.dynamic_index_in_dim(near_blocks, c, 0, keepdims=False)
    came = [own_block, send(near_blocks, 1)] + from_far
    came = [lax.select_n(place, *[came[i ^ j] for j in range(4)]) for i in range(4)]
    outputs = jnp.stack(
        [block.reshape(4, STEPS, PROMPT_DEV, FEATURES) for block in came], axis=1
    )
    outputs = outputs.transpose(2, 0, 1, 3, 4).reshape(STEPS, 16 * PROMPT_DEV, FEATURES)
    return (
        qkv_updated,
        out_updated,
        qkv_moment_next,
        out_moment_next,
        qkv_second_next,
        out_second_next,
        outputs,
    )


def solution(mesh):
    fine = Mesh(mesh.devices.reshape(SIZES), AXES)
    rows = P(AXES, None)
    caches = P(AXES, None, None, None)
    states = P(None, ("xh", "y"), ("z", "xl", "c"))
    return jax.shard_map(
        on_device,
        mesh=fine,
        in_specs=(rows,) * 8 + (states, caches, caches, P(AXES)),
        out_specs=(rows,) * 6 + (states,),
        check_vma=False,
    )
```
